32 devices in a mesh: cd: 8 (over y, x, core), ab: 4 (over z).
Axes of the slice: x: 2, y: 2, z: 4, core: 2. Of those that a mesh axis runs over, the one named last changes fastest.
Arguments:
- amplitudes: float32 [1024, 16384], P('ab', 'cd'), may hold values from -6 to 6
- integrals: float32 [16384, 4096], P('cd', 'ab'), may hold values from -0.046875 to 0.046875
- live_tiles: int32 [64], P('cd'), may hold values from 0 to 1, as said below
- residual_in: float32 [1024, 4096], P(('ab', 'cd')), may hold values from -6 to 6
Outputs:
- residual_out: float32 [1024, 4096], P(('ab', 'cd'))
The draws below stay inside these ranges and needn't reach their ends.
Inputs may be any that keep to these rules, and one draw needn't show every extreme that they name: live_tiles[t] is 1 where tile t of 256 contracted pairs carries integrals and 0 where it is screened out; the 8 tiles of each index of cd hold at least one live tile.
All inputs are finite; a program needn't handle non-finite values.
Results may differ from the reference program's by a relative error of at most 0.0001.
Values sent between devices are 32-bit elements; how exact they have to be, the bound alone decides.
No kernel may reach another device: no remote copies, remote signals or barrier semaphores. Data moves between devices by JAX's collectives and lax.ppermute only.
A program may use at most 128 MiB of HBM per device.

```python
import jax
import jax.numpy as jnp
from jax import lax

IJ = 1024
AB = 4096
TILE = 256
CD_DEV = 2048
TILES_DEV = 8
CD = 16384
N_CD = 8


def draw_live_tiles(key, part):
    key = jax.random.fold_in(key, 11)
    groups = CD // TILE // TILES_DEV
    count_key, order_key = jax.random.split(key)
    counts = jax.random.randint(count_key, (groups, 1), 1, TILES_DEV + 1)
    order_keys = jax.random.split(order_key, groups)
    orders = jax.vmap(lambda single: jax.random.permutation(single, TILES_DEV))(order_keys)
    return (orders < counts).astype(jnp.int32).reshape(-1)


def shard_levels(key, shape, cuts, least, high):
    def one(axis_at, shards_of):
        steps = jax.random.uniform(jax.random.fold_in(jax.random.fold_in(key, 6), axis_at), (shards_of,), jnp.float32, least / len(cuts), high / len(cuts))
        return jnp.repeat(jnp.exp(steps), shape[axis_at] // shards_of).reshape((-1,) + (1,) * (len(shape) - axis_at - 1))

    factor_of = one(*cuts[0])
    for cut in cuts[1:]:
        factor_of = factor_of * one(*cut)
    return factor_of


def centred(key, extent, deviation, bound, cuts=(), dtype=jnp.bfloat16):
    result = deviation * jax.random.normal(key, extent, jnp.float32)
    if cuts:
        result = result * shard_levels(key, extent, cuts, -0.22, 0.18)
    return jnp.clip(result, -bound, bound).astype(dtype)


def setup_inputs(seed: int = 0) -> dict:
    keys = jax.random.split(jax.random.key(seed), 5)
    amplitudes = centred(keys[0], (IJ, CD), 1.0, 6.0, ((0, 4), (1, 8)), jnp.float32)
    integrals = centred(keys[1], (CD, AB), CD ** -0.5, 0.046875, ((0, 8), (1, 4)), jnp.float32)
    live_tiles = draw_live_tiles(jax.random.fold_in(keys[4], 71), 0)
    residual_in = centred(keys[3], (IJ, AB), 1.0, 6.0, ((0, 32),), jnp.float32)
    return {"amplitudes": amplitudes, "integrals": integrals, "live_tiles": live_tiles, "residual_in": residual_in}


def reference(amplitudes, integrals, live_tiles, residual_in):
    def add_block(block, total):
        first = (block * CD_DEV).astype(jnp.int32)
        left_part = lax.dynamic_slice_in_dim(amplitudes, first, CD_DEV, 1)
        right_part = lax.dynamic_slice_in_dim(integrals, first, CD_DEV, 0)
        flag_first = (block * TILES_DEV).astype(jnp.int32)
        flags = lax.dynamic_slice_in_dim(live_tiles, flag_first, TILES_DEV, 0)
        weights = jnp.repeat(flags.astype(jnp.float32), TILE, total_repeat_length=CD_DEV)
        return total + jnp.dot(left_part, right_part * weights[:, None], preferred_element_type=jnp.float32, precision=lax.Precision.HIGHEST)

    ladder = lax.fori_loop(jnp.int32(0), jnp.int32(N_CD), add_block, jnp.zeros((IJ, AB), jnp.float32))
    return residual_in + ladder
```

```python
import functools

import jax
import jax.numpy as jnp
from jax import lax
from jax.experimental import pallas as pl
from jax.experimental.pallas import tpu as pltpu
from jax.sharding import PartitionSpec as P

TILE = 256
MIB = 1 << 20


def split(x):
    high = x.astype(jnp.bfloat16)
    return high, (x - high.astype(jnp.float32)).astype(jnp.bfloat16)


def multiply_add(out_ref, left, high, low):
    left_high, left_low = split(left)
    dot = functools.partial(jnp.dot, preferred_element_type=jnp.float32)
    both = dot(jnp.concatenate([left_high, left_low]), high)
    rows = left.shape[0]
    out_ref[...] += both[:rows] + (both[rows:] + dot(left_high, low))


def first_kernel(live, left_ref, right_ref, out_ref, high_ref, low_ref):
    step = pl.program_id(0)

    @pl.when(step == 0)
    def _():
        out_ref[...] = jnp.zeros_like(out_ref)

    @pl.when(live[step] > 0)
    def _():
        high_ref[0], low_ref[0] = split(right_ref[0])
        multiply_add(out_ref, left_ref[...], high_ref[0], low_ref[0])


def first_product(left, right, live):
    rows = left.shape[0]
    steps, _, columns = right.shape
    tile = pl.BlockSpec((1, TILE, columns), lambda step, live: (step, 0, 0))
    halved = jax.ShapeDtypeStruct(right.shape, jnp.bfloat16)
    return pl.pallas_call(
        first_kernel,
        out_shape=(jax.ShapeDtypeStruct((rows, columns), jnp.float32), halved, halved),
        grid_spec=pltpu.PrefetchScalarGridSpec(
            num_scalar_prefetch=1,
            grid=(steps,),
            in_specs=[pl.BlockSpec((rows, TILE), lambda step, live: (0, step)), tile],
            out_specs=(pl.BlockSpec((rows, columns), lambda step, live: (0, 0)), tile, tile),
        ),
        compiler_params=pltpu.CompilerParams(vmem_limit_bytes=16 * MIB),
        cost_estimate=pl.CostEstimate(
            flops=2 * rows * TILE * columns * steps,
            bytes_accessed=4 * rows * (steps * TILE + columns),
            transcendentals=0,
        ),
    )(live, left, right)


def product_kernel(layout, first, scalars, *refs):
    count = len(layout)
    left_refs, (high_ref, low_ref, out_ref, *lefts) = refs[: sum(layout)], refs[sum(layout) :]
    lefts, (high, low, left_sems, sems) = lefts[:count], lefts[count:]
    steps = high.shape[0]

    left_copies = []
    for i, candidates in enumerate(layout):
        here, left_refs = left_refs[:candidates], left_refs[candidates:]
        copies = [pltpu.make_async_copy(ref, lefts[i], left_sems.at[i]) for ref in here]
        if candidates == 1:
            copies[0].start()
        else:
            for which, copy in enumerate(copies):
                pl.when(scalars[0] == which)(copy.start)
        left_copies.append(copies[0])
    right_copies = []
    for step in range(steps):
        pairs = (high_ref, high), (low_ref, low)
        right_copies.append(
            [
                pltpu.make_async_copy(source.at[first + step], target.at[step], sems.at[i, step])
                for i, (source, target) in enumerate(pairs)
            ]
        )
        for copy in right_copies[-1]:
            copy.start()
    out_ref[...] = jnp.zeros_like(out_ref)

    step = 0
    for i, left in enumerate(lefts):
        left_copies[i].wait()
        for tile in range(left.shape[1] // TILE):
            for copy in right_copies[step]:
                copy.wait()

            @pl.when(scalars[1 + step] > 0)
            def _():
                left_tile = left[:, tile * TILE : (tile + 1) * TILE]
                multiply_add(out_ref, left_tile, high[step], low[step])

            step += 1


def product(lists, which, right, live, first=0):
    rows, columns = lists[0][0].shape[0], right[0].shape[2]
    widths = [candidates[0].shape[1] for candidates in lists]
    steps = sum(widths) // TILE
    lefts = [x for candidates in lists for x in candidates]
    anywhere, hbm = (pl.BlockSpec(memory_space=space) for space in (pl.ANY, pltpu.HBM))
    return pl.pallas_call(
        functools.partial(product_kernel, [len(candidates) for candidates in lists], first),
        out_shape=jax.ShapeDtypeStruct((rows, columns), jnp.float32),
        in_specs=[pl.BlockSpec(memory_space=pltpu.SMEM)] + [anywhere] * len(lefts) + [hbm] * 2,
        out_specs=pl.BlockSpec(memory_space=pltpu.VMEM),
        scratch_shapes=[pltpu.VMEM((rows, width), jnp.float32) for width in widths]
        + [
            pltpu.VMEM((steps, TILE, columns), jnp.bfloat16),
            pltpu.VMEM((steps, TILE, columns), jnp.bfloat16),
            pltpu.SemaphoreType.DMA((len(lists),)),
            pltpu.SemaphoreType.DMA((2, steps)),
        ],
        compiler_params=pltpu.CompilerParams(vmem_limit_bytes=52 * MIB),
        cost_estimate=pl.CostEstimate(
            flops=2 * rows * TILE * columns * steps,
            bytes_accessed=4 * rows * (steps * TILE + columns),
            transcendentals=0,
        ),
    )(jnp.concatenate([jnp.int32(which)[None], live[first : first + steps]]), *lefts, *right)


def cut(left, tiles):
    kept = (tiles - tiles // 4) * TILE
    return [left[:, :kept], left[:, kept:]]


def take(blocks, at, axis):
    return lax.dynamic_index_in_dim(blocks, at, axis, keepdims=False)


def halve(blocks, axis, bit):
    mine = (lax.axis_index("cd") >> bit) & 1
    pairs = [(i, i ^ (1 << bit)) for i in range(lax.axis_size("cd"))]
    return take(blocks, mine, axis) + lax.ppermute(take(blocks, 1 - mine, axis), "cd", pairs)


def core_sum(partial_rows):
    count = lax.axis_size("cd")
    rows, columns = partial_rows.shape
    return halve(partial_rows.reshape(count // 2, 2, rows // count, columns), 1, 0)


def chip_sum(blocks):
    bit = 1
    while blocks.shape[0] > 1:
        chips, rows, columns = blocks.shape
        blocks = halve(blocks.reshape(chips // 2, 2, rows, columns), 1, bit)
        bit += 1
    return blocks[0]


def chip_sum_direct(blocks):
    chip, count = lax.axis_index("cd") // 2, lax.axis_size("cd")
    total = take(blocks, chip, 0)
    for flip in range(1, blocks.shape[0]):
        pairs = [(i, i ^ (2 * flip)) for i in range(count)]
        total += lax.ppermute(take(blocks, chip ^ flip, 0), "cd", pairs)
    return total


def send(x, pairs):
    return lax.ppermute(x, "ab", pairs)


def after(*values):
    return lax.optimization_barrier(values)


def ladder_any(amplitudes, live, right):
    count = lax.axis_size("ab")
    first, *split_right = first_product(amplitudes, right, live)
    home = [chip_sum(core_sum(first))]
    for flip in range(1, count):
        pairs = [(i, i ^ flip) for i in range(count)]
        lists = [[send(x, pairs)] for x in cut(amplitudes, live.shape[0])]
        partial_rows = product(lists, 0, split_right, live)
        home.append(send(chip_sum(core_sum(partial_rows)), pairs))
    return [take(jnp.stack(home), lax.axis_index("ab") ^ i, 0) for i in range(count)]


def ladder_line(amplitudes, live, right):
    at = lax.axis_index("ab")
    inner = ((at == 1) | (at == 2)).astype(jnp.int32)
    swap_1 = [(0, 1), (1, 0), (2, 3), (3, 2)]
    swap_2 = [(0, 2), (2, 0), (1, 3), (3, 1)]
    swap_3 = [(0, 3), (3, 0), (1, 2), (2, 1)]
    swap_inner, to_end = [(1, 2), (2, 1)], [(1, 0), (2, 3)]
    lists = cut(amplitudes, live.shape[0])
    kept = lists[0].shape[1] // TILE

    one = [send(x, swap_1) for x in lists]
    three_inner = [send(x, swap_inner) for x in lists]
    two_inner = [send(x, swap_inner) for x in one]
    two_end = [send(x, to_end) for x in three_inner]
    three_end = [send(x, to_end) for x in two_inner]

    first, *split_right = first_product(amplitudes, right, live)
    sum_0 = core_sum(first)

    one[0], three_inner[0], sum_0 = after(one[0], three_inner[0], sum_0)
    one[1], three_inner[1], sum_0 = after(one[1], three_inner[1], sum_0)
    sum_1 = core_sum(product([[x] for x in one], 0, split_right, live))
    home_0 = chip_sum(sum_0)

    two_end[0], two_inner[0], home_0, sum_1 = after(two_end[0], two_inner[0], home_0, sum_1)
    two_end[1], two_inner[1], sum_1 = after(two_end[1], two_inner[1], sum_1)
    candidates = [list(pair) for pair in zip(two_end, two_inner)]
    sum_2 = core_sum(product(candidates, inner, split_right, live))
    sum_1 = chip_sum(sum_1)

    three_end[0], sum_1, sum_2 = after(three_end[0], sum_1, sum_2)
    candidates = [[three_end[0], three_inner[0]]]
    partial_3 = product(candidates, inner, split_right, live)
    sum_2 = chip_sum_direct(sum_2)
    home_1 = send(sum_1, swap_1)

    three_end[1], partial_3, sum_2, home_1 = after(three_end[1], partial_3, sum_2, home_1)
    candidates = [[three_end[1], three_inner[1]]]
    partial_3 += product(candidates, inner, split_right, live, kept)
    sum_3 = chip_sum_direct(core_sum(partial_3))
    home_2 = send(sum_2, swap_2)

    home_2, sum_3 = after(home_2, sum_3)
    home = jnp.stack([home_0, home_1, home_2, send(sum_3, swap_3)])
    return [take(home, at ^ i, 0) for i in range(4)]


def per_device(amplitudes, integrals, live_tiles, residual_in):
    right = integrals.reshape(live_tiles.shape[0], TILE, integrals.shape[1])
    ladder = ladder_line if lax.axis_size("ab") == 4 else ladder_any
    return residual_in + jnp.concatenate(ladder(amplitudes, live_tiles, right), axis=1)


def solution(mesh):
    return jax.shard_map(
        per_device,
        mesh=mesh,
        in_specs=(P("ab", "cd"), P("cd", "ab"), P("cd"), P(("ab", "cd"), None)),
        out_specs=P(("ab", "cd"), None),
        check_vma=False,
    )
```

```python
import functools

import jax
import jax.numpy as jnp
from jax import lax
from jax.experimental import pallas as pl
from jax.experimental.pallas import tpu as pltpu
from jax.sharding import PartitionSpec as P

TILE = 256
MIB = 1 << 20


def split(x):
    high = x.astype(jnp.bfloat16)
    return high, (x - high.astype(jnp.float32)).astype(jnp.bfloat16)


def multiply_add(out_ref, left, high, low):
    left_high, left_low = split(left)
    dot = functools.partial(jnp.dot, preferred_element_type=jnp.float32)
    both = dot(jnp.concatenate([left_high, left_low]), high)
    rows = left.shape[0]
    out_ref[...] += both[:rows] + (both[rows:] + dot(left_high, low))


def first_kernel(live, left_ref, right_ref, out_ref, high_ref, low_ref):
    step = pl.program_id(0)

    @pl.when(step == 0)
    def _():
        out_ref[...] = jnp.zeros_like(out_ref)

    @pl.when(live[step] > 0)
    def _():
        high_ref[0], low_ref[0] = split(right_ref[0])
        multiply_add(out_ref, left_ref[...], high_ref[0], low_ref[0])


def first_product(left, right, live):
    rows = left.shape[0]
    steps, _, columns = right.shape
    tile = pl.BlockSpec((1, TILE, columns), lambda step, live: (step, 0, 0))
    halved = jax.ShapeDtypeStruct(right.shape, jnp.bfloat16)
    return pl.pallas_call(
        first_kernel,
        out_shape=(jax.ShapeDtypeStruct((rows, columns), jnp.float32), halved, halved),
        grid_spec=pltpu.PrefetchScalarGridSpec(
            num_scalar_prefetch=1,
            grid=(steps,),
            in_specs=[pl.BlockSpec((rows, TILE), lambda step, live: (0, step)), tile],
            out_specs=(pl.BlockSpec((rows, columns), lambda step, live: (0, 0)), tile, tile),
        ),
        compiler_params=pltpu.CompilerParams(vmem_limit_bytes=16 * MIB),
        cost_estimate=pl.CostEstimate(
            flops=2 * rows * TILE * columns * steps,
            bytes_accessed=4 * rows * (steps * TILE + columns),
            transcendentals=0,
        ),
    )(live, left, right)


def product_kernel(layout, added, scalars, *refs):
    count = len(layout)
    left_refs, refs = refs[: sum(layout)], refs[sum(layout) :]
    (high_ref, low_ref), refs = refs[:2], refs[2:]
    added_ref, (out_ref, *lefts) = (refs[0], refs[1:]) if added else (None, refs)
    lefts, (high, low, left_sems, sems) = lefts[:count], lefts[count:]
    steps = high.shape[0]

    left_copies = []
    for i, candidates in enumerate(layout):
        here, left_refs = left_refs[:candidates], left_refs[candidates:]
        copies = [pltpu.make_async_copy(ref, lefts[i], left_sems.at[i]) for ref in here]
        if candidates == 1:
            copies[0].start()
        else:
            for which, copy in enumerate(copies):
                pl.when(scalars[0] == which)(copy.start)
        left_copies.append(copies[0])
    right_copies = []
    for step in range(steps):
        pairs = (high_ref, high), (low_ref, low)
        right_copies.append(
            [
                pltpu.make_async_copy(source.at[step], target.at[step], sems.at[i, step])
                for i, (source, target) in enumerate(pairs)
            ]
        )
        for copy in right_copies[-1]:
            copy.start()
    out_ref[...] = added_ref[...] if added else jnp.zeros_like(out_ref)

    step = 0
    for i, left in enumerate(lefts):
        left_copies[i].wait()
        for tile in range(left.shape[1] // TILE):
            for copy in right_copies[step]:
                copy.wait()

            @pl.when(scalars[1 + step] > 0)
            def _():
                left_tile = left[:, tile * TILE : (tile + 1) * TILE]
                multiply_add(out_ref, left_tile, high[step], low[step])

            step += 1


def product(lists, which, right, live, added=None):
    rows, columns = lists[0][0].shape[0], right[0].shape[2]
    widths = [candidates[0].shape[1] for candidates in lists]
    steps = sum(widths) // TILE
    lefts = [x for candidates in lists for x in candidates]
    anywhere, vmem = (pl.BlockSpec(memory_space=space) for space in (pl.ANY, pltpu.VMEM))
    more = [] if added is None else [added]
    return pl.pallas_call(
        functools.partial(product_kernel, [len(candidates) for candidates in lists], added is not None),
        out_shape=jax.ShapeDtypeStruct((rows, columns), jnp.float32),
        in_specs=[pl.BlockSpec(memory_space=pltpu.SMEM)]
        + [anywhere] * (len(lefts) + 2)
        + [vmem] * len(more),
        out_specs=pl.BlockSpec(memory_space=pltpu.VMEM),
        scratch_shapes=[pltpu.VMEM((rows, width), jnp.float32) for width in widths]
        + [
            pltpu.VMEM((steps, TILE, columns), jnp.bfloat16),
            pltpu.VMEM((steps, TILE, columns), jnp.bfloat16),
            pltpu.SemaphoreType.DMA((len(lists),)),
            pltpu.SemaphoreType.DMA((2, steps)),
        ],
        compiler_params=pltpu.CompilerParams(vmem_limit_bytes=(52 if steps > 2 else 10) * MIB),
        cost_estimate=pl.CostEstimate(
            flops=2 * rows * TILE * columns * steps,
            bytes_accessed=4 * rows * (steps * TILE + columns),
            transcendentals=0,
        ),
    )(jnp.concatenate([jnp.int32(which)[None], live[:steps]]), *lefts, *right, *more)


def cut(left, tiles):
    kept = (tiles - tiles // 4) * TILE
    return [left[:, :kept], left[:, kept:]]


def take(blocks, at, axis):
    return lax.dynamic_index_in_dim(blocks, at, axis, keepdims=False)


def halve(blocks, axis, bit):
    mine = (lax.axis_index("cd") >> bit) & 1
    pairs = [(i, i ^ (1 << bit)) for i in range(lax.axis_size("cd"))]
    return take(blocks, mine, axis) + lax.ppermute(take(blocks, 1 - mine, axis), "cd", pairs)


def core_sum(partial_rows):
    count = lax.axis_size("cd")
    rows, columns = partial_rows.shape
    return halve(partial_rows.reshape(count // 2, 2, rows // count, columns), 1, 0)


def chip_sum(blocks):
    bit = 1
    while blocks.shape[0] > 1:
        chips, rows, columns = blocks.shape
        blocks = halve(blocks.reshape(chips // 2, 2, rows, columns), 1, bit)
        bit += 1
    return blocks[0]


def chip_sum_direct(blocks):
    chip, count = lax.axis_index("cd") // 2, lax.axis_size("cd")
    total = take(blocks, chip, 0)
    for flip in range(1, blocks.shape[0]):
        pairs = [(i, i ^ (2 * flip)) for i in range(count)]
        total += lax.ppermute(take(blocks, chip ^ flip, 0), "cd", pairs)
    return total


def send(x, pairs):
    return lax.ppermute(x, "ab", pairs)


def after(*values):
    return lax.optimization_barrier(values)


def ladder_any(amplitudes, live, right):
    count = lax.axis_size("ab")
    first, *split_right = first_product(amplitudes, right, live)
    home = [chip_sum(core_sum(first))]
    for flip in range(1, count):
        pairs = [(i, i ^ flip) for i in range(count)]
        lists = [[send(x, pairs)] for x in cut(amplitudes, live.shape[0])]
        partial_rows = product(lists, 0, split_right, live)
        home.append(send(chip_sum(core_sum(partial_rows)), pairs))
    return [take(jnp.stack(home), lax.axis_index("ab") ^ i, 0) for i in range(count)]


def ladder_line(amplitudes, live, right):
    at = lax.axis_index("ab")
    inner = ((at == 1) | (at == 2)).astype(jnp.int32)
    swap_1 = [(0, 1), (1, 0), (2, 3), (3, 2)]
    swap_2 = [(0, 2), (2, 0), (1, 3), (3, 1)]
    swap_3 = [(0, 3), (3, 0), (1, 2), (2, 1)]
    swap_inner, to_end = [(1, 2), (2, 1)], [(1, 0), (2, 3)]
    lists = cut(amplitudes, live.shape[0])
    kept = lists[0].shape[1] // TILE

    one = [send(x, swap_1) for x in lists]
    three_inner = [send(x, swap_inner) for x in lists]
    two_inner = [send(x, swap_inner) for x in one]
    two_end = [send(x, to_end) for x in three_inner]
    three_end = [send(x, to_end) for x in two_inner]

    first, *split_right = first_product(amplitudes, right, live)
    sum_0 = core_sum(first)

    one[0], three_inner[0], sum_0 = after(one[0], three_inner[0], sum_0)
    one[1], three_inner[1], sum_0 = after(one[1], three_inner[1], sum_0)
    sum_1 = core_sum(product([[x] for x in one], 0, split_right, live))
    home_0 = chip_sum(sum_0)

    two_end[0], two_inner[0], home_0, sum_1 = after(two_end[0], two_inner[0], home_0, sum_1)
    two_end[1], two_inner[1], sum_1 = after(two_end[1], two_inner[1], sum_1)
    candidates = [list(pair) for pair in zip(two_end, two_inner)]
    sum_2 = core_sum(product(candidates, inner, split_right, live))
    sum_1 = chip_sum(sum_1)

    last_right = [x[kept:] for x in split_right]

    three_end[0], sum_1, sum_2, last_right = after(three_end[0], sum_1, sum_2, last_right)
    candidates = [[three_end[0], three_inner[0]]]
    partial_3 = product(candidates, inner, split_right, live)
    sum_2 = chip_sum_direct(sum_2)
    home_1 = send(sum_1, swap_1)

    three_end[1], partial_3, sum_2, home_1 = after(three_end[1], partial_3, sum_2, home_1)
    candidates = [[three_end[1], three_inner[1]]]
    partial_3 = product(candidates, inner, last_right, live[kept:], partial_3)
    sum_3 = chip_sum_direct(core_sum(partial_3))
    home_2 = send(sum_2, swap_2)

    home_2, sum_3 = after(home_2, sum_3)
    home = jnp.stack([home_0, home_1, home_2, send(sum_3, swap_3)])
    return [take(home, at ^ i, 0) for i in range(4)]


def per_device(amplitudes, integrals, live_tiles, residual_in):
    right = integrals.reshape(live_tiles.shape[0], TILE, integrals.shape[1])
    ladder = ladder_line if lax.axis_size("ab") == 4 else ladder_any
    return residual_in + jnp.concatenate(ladder(amplitudes, live_tiles, right), axis=1)


def solution(mesh):
    return jax.shard_map(
        per_device,
        mesh=mesh,
        in_specs=(P("ab", "cd"), P("cd", "ab"), P("cd"), P(("ab", "cd"), None)),
        out_specs=P(("ab", "cd"), None),
        check_vma=False,
    )
```

```python
import functools

import jax
import jax.numpy as jnp
from jax import lax
from jax.experimental import pallas as pl
from jax.experimental.pallas import tpu as pltpu
from jax.sharding import PartitionSpec as P

TILE = 256
MIB = 1 << 20


def split(x):
    high = x.astype(jnp.bfloat16)
    return high, (x - high.astype(jnp.float32)).astype(jnp.bfloat16)


def multiply_add(out_ref, left, high, low):
    left_high, left_low = split(left)
    dot = functools.partial(jnp.dot, preferred_element_type=jnp.float32)
    both = dot(jnp.concatenate([left_high, left_low]), high)
    rows = left.shape[0]
    out_ref[...] += both[:rows] + (both[rows:] + dot(left_high, low))


def first_kernel(live, left_ref, right_ref, out_ref, high_ref, low_ref):
    step = pl.program_id(0)

    @pl.when(step == 0)
    def _():
        out_ref[...] = jnp.zeros_like(out_ref)

    @pl.when(live[step] > 0)
    def _():
        high_ref[0], low_ref[0] = split(right_ref[0])
        multiply_add(out_ref, left_ref[...], high_ref[0], low_ref[0])


def first_product(left, right, live):
    rows = left.shape[0]
    steps, _, columns = right.shape
    tile = pl.BlockSpec((1, TILE, columns), lambda step, live: (step, 0, 0))
    halved = jax.ShapeDtypeStruct(right.shape, jnp.bfloat16)
    return pl.pallas_call(
        first_kernel,
        out_shape=(jax.ShapeDtypeStruct((rows, columns), jnp.float32), halved, halved),
        grid_spec=pltpu.PrefetchScalarGridSpec(
            num_scalar_prefetch=1,
            grid=(steps,),
            in_specs=[pl.BlockSpec((rows, TILE), lambda step, live: (0, step)), tile],
            out_specs=(pl.BlockSpec((rows, columns), lambda step, live: (0, 0)), tile, tile),
        ),
        compiler_params=pltpu.CompilerParams(vmem_limit_bytes=16 * MIB),
        cost_estimate=pl.CostEstimate(
            flops=2 * rows * TILE * columns * steps,
            bytes_accessed=4 * rows * (steps * TILE + columns),
            transcendentals=0,
        ),
    )(live, left, right)


def product_kernel(layout, added, scalars, *refs):
    count = len(layout)
    left_refs, refs = refs[: sum(layout)], refs[sum(layout) :]
    (high_ref, low_ref), refs = refs[:2], refs[2:]
    added_ref, (out_ref, *lefts) = (refs[0], refs[1:]) if added else (None, refs)
    lefts, (high, low, left_sems, sems) = lefts[:count], lefts[count:]
    steps = high.shape[0]

    left_copies = []
    for i, candidates in enumerate(layout):
        here, left_refs = left_refs[:candidates], left_refs[candidates:]
        copies = [pltpu.make_async_copy(ref, lefts[i], left_sems.at[i]) for ref in here]
        if candidates == 1:
            copies[0].start()
        else:
            for which, copy in enumerate(copies):
                pl.when(scalars[0] == which)(copy.start)
        left_copies.append(copies[0])
    right_copies = []
    for step in range(steps):
        pairs = (high_ref, high), (low_ref, low)
        right_copies.append(
            [
                pltpu.make_async_copy(source.at[step], target.at[step], sems.at[i, step])
                for i, (source, target) in enumerate(pairs)
            ]
        )
        for copy in right_copies[-1]:
            copy.start()
    out_ref[...] = added_ref[...] if added else jnp.zeros_like(out_ref)

    step = 0
    for i, left in enumerate(lefts):
        left_copies[i].wait()
        for tile in range(left.shape[1] // TILE):
            for copy in right_copies[step]:
                copy.wait()

            @pl.when(scalars[1 + step] > 0)
            def _():
                left_tile = left[:, tile * TILE : (tile + 1) * TILE]
                multiply_add(out_ref, left_tile, high[step], low[step])

            step += 1


def product(lists, which, right, live, added=None):
    rows, columns = lists[0][0].shape[0], right[0].shape[2]
    widths = [candidates[0].shape[1] for candidates in lists]
    steps = sum(widths) // TILE
    lefts = [x for candidates in lists for x in candidates]
    anywhere, vmem = (pl.BlockSpec(memory_space=space) for space in (pl.ANY, pltpu.VMEM))
    more = [] if added is None else [added]
    return pl.pallas_call(
        functools.partial(product_kernel, [len(candidates) for candidates in lists], added is not None),
        out_shape=jax.ShapeDtypeStruct((rows, columns), jnp.float32),
        in_specs=[pl.BlockSpec(memory_space=pltpu.SMEM)]
        + [anywhere] * (len(lefts) + 2)
        + [vmem] * len(more),
        out_specs=pl.BlockSpec(memory_space=pltpu.VMEM),
        scratch_shapes=[pltpu.VMEM((rows, width), jnp.float32) for width in widths]
        + [
            pltpu.VMEM((steps, TILE, columns), jnp.bfloat16),
            pltpu.VMEM((steps, TILE, columns), jnp.bfloat16),
            pltpu.SemaphoreType.DMA((len(lists),)),
            pltpu.SemaphoreType.DMA((2, steps)),
        ],
        compiler_params=pltpu.CompilerParams(vmem_limit_bytes=(52 if steps > 2 else 10) * MIB),
        cost_estimate=pl.CostEstimate(
            flops=2 * rows * TILE * columns * steps,
            bytes_accessed=4 * rows * (steps * TILE + columns),
            transcendentals=0,
        ),
    )(jnp.concatenate([jnp.int32(which)[None], live[:steps]]), *lefts, *right, *more)


def cut(left, tiles):
    kept = (tiles - tiles // 4) * TILE
    return [left[:, :kept], left[:, kept:]]


def take(blocks, at, axis):
    return lax.dynamic_index_in_dim(blocks, at, axis, keepdims=False)


def halve(blocks, axis, bit):
    mine = (lax.axis_index("cd") >> bit) & 1
    pairs = [(i, i ^ (1 << bit)) for i in range(lax.axis_size("cd"))]
    return take(blocks, mine, axis) + lax.ppermute(take(blocks, 1 - mine, axis), "cd", pairs)


def core_sum(partial_rows):
    count = lax.axis_size("cd")
    rows, columns = partial_rows.shape
    return halve(partial_rows.reshape(count // 2, 2, rows // count, columns), 1, 0)


def chip_sum(blocks):
    bit = 1
    while blocks.shape[0] > 1:
        chips, rows, columns = blocks.shape
        blocks = halve(blocks.reshape(chips // 2, 2, rows, columns), 1, bit)
        bit += 1
    return blocks[0]


def chip_sum_direct(blocks):
    chip, count = lax.axis_index("cd") // 2, lax.axis_size("cd")
    total = take(blocks, chip, 0)
    for flip in range(1, blocks.shape[0]):
        pairs = [(i, i ^ (2 * flip)) for i in range(count)]
        total += lax.ppermute(take(blocks, chip ^ flip, 0), "cd", pairs)
    return total


def send(x, pairs):
    return lax.ppermute(x, "ab", pairs)


def after(*values):
    return lax.optimization_barrier(values)


def place(home):
    at, parts = lax.axis_index("ab"), []
    for i in range(len(home)):
        part = home[0]
        for flip in range(1, len(home)):
            part = jnp.where(at ^ i == flip, home[flip], part)
        parts.append(part)
    return jnp.concatenate(parts, axis=1)


def ladder_any(amplitudes, live, right):
    count = lax.axis_size("ab")
    first, *split_right = first_product(amplitudes, right, live)
    home = [chip_sum(core_sum(first))]
    for flip in range(1, count):
        pairs = [(i, i ^ flip) for i in range(count)]
        lists = [[send(x, pairs)] for x in cut(amplitudes, live.shape[0])]
        partial_rows = product(lists, 0, split_right, live)
        home.append(send(chip_sum(core_sum(partial_rows)), pairs))
    return place(home)


def ladder_line(amplitudes, live, right):
    at = lax.axis_index("ab")
    inner = ((at == 1) | (at == 2)).astype(jnp.int32)
    swap_1 = [(0, 1), (1, 0), (2, 3), (3, 2)]
    swap_2 = [(0, 2), (2, 0), (1, 3), (3, 1)]
    swap_3 = [(0, 3), (3, 0), (1, 2), (2, 1)]
    swap_inner, to_end = [(1, 2), (2, 1)], [(1, 0), (2, 3)]
    tiles = live.shape[0]
    kept = tiles - tiles // 4

    one, three_inner = send(amplitudes, swap_1), send(amplitudes, swap_inner)
    two_end = send(three_inner, to_end)
    two_inner = [send(x, swap_inner) for x in cut(one, tiles)]
    three_end = [send(x, to_end) for x in two_inner]

    first, *split_right = first_product(amplitudes, right, live)
    sum_0 = core_sum(first)

    one, three_inner, sum_0 = after(one, three_inner, sum_0)
    three_inner = cut(three_inner, tiles)
    sum_1 = core_sum(product([[one]], 0, split_right, live))
    home_0 = chip_sum(sum_0)

    two_inner[0], home_0, sum_1 = after(two_inner[0], home_0, sum_1)
    two_end, two_inner[1], three_inner, sum_1 = after(two_end, two_inner[1], three_inner, sum_1)
    two_end = cut(two_end, tiles)
    candidates = [list(pair) for pair in zip(two_end, two_inner)]
    sum_2 = core_sum(product(candidates, inner, split_right, live))
    sum_1 = chip_sum(sum_1)

    last_right = [x[kept:] for x in split_right]

    three_end[0], sum_1, sum_2, last_right = after(three_end[0], sum_1, sum_2, last_right)
    candidates = [[three_end[0], three_inner[0]]]
    partial_3 = product(candidates, inner, split_right, live)
    sum_2 = chip_sum_direct(sum_2)
    home_1 = send(sum_1, swap_1)

    three_end[1], partial_3, sum_2, home_1 = after(three_end[1], partial_3, sum_2, home_1)
    candidates = [[three_end[1], three_inner[1]]]
    partial_3 = product(candidates, inner, last_right, live[kept:], partial_3)
    sum_3 = chip_sum_direct(core_sum(partial_3))
    home_2 = send(sum_2, swap_2)

    home_2, sum_3 = after(home_2, sum_3)
    return place([home_0, home_1, home_2, send(sum_3, swap_3)])


def per_device(amplitudes, integrals, live_tiles, residual_in):
    right = integrals.reshape(live_tiles.shape[0], TILE, integrals.shape[1])
    ladder = ladder_line if lax.axis_size("ab") == 4 else ladder_any
    return residual_in + ladder(amplitudes, live_tiles, right)


def solution(mesh):
    return jax.shard_map(
        per_device,
        mesh=mesh,
        in_specs=(P("ab", "cd"), P("cd", "ab"), P("cd"), P(("ab", "cd"), None)),
        out_specs=P(("ab", "cd"), None),
        check_vma=False,
    )
```

```python
import functools

import jax
import jax.numpy as jnp
from jax import lax
from jax.experimental import pallas as pl
from jax.experimental.pallas import tpu as pltpu
from jax.sharding import PartitionSpec as P

TILE = 256
MIB = 1 << 20


def split(x):
    high = x.astype(jnp.bfloat16)
    return high, (x - high.astype(jnp.float32)).astype(jnp.bfloat16)


def multiply_add(out_ref, left, high, low):
    left_high, left_low = split(left)
    dot = functools.partial(jnp.dot, preferred_element_type=jnp.float32)
    both = dot(jnp.concatenate([left_high, left_low]), high)
    rows = left.shape[0]
    out_ref[...] += both[:rows] + (both[rows:] + dot(left_high, low))


def first_kernel(live, left_ref, right_ref, out_ref, high_ref, low_ref):
    step = pl.program_id(0)

    @pl.when(step == 0)
    def _():
        out_ref[...] = jnp.zeros_like(out_ref)

    @pl.when(live[step] > 0)
    def _():
        high_ref[0], low_ref[0] = split(right_ref[0])
        multiply_add(out_ref, left_ref[...], high_ref[0], low_ref[0])


def first_product(left, right, live):
    rows = left.shape[0]
    steps, _, columns = right.shape
    tile = pl.BlockSpec((1, TILE, columns), lambda step, live: (step, 0, 0))
    halved = jax.ShapeDtypeStruct(right.shape, jnp.bfloat16)
    return pl.pallas_call(
        first_kernel,
        out_shape=(jax.ShapeDtypeStruct((rows, columns), jnp.float32), halved, halved),
        grid_spec=pltpu.PrefetchScalarGridSpec(
            num_scalar_prefetch=1,
            grid=(steps,),
            in_specs=[pl.BlockSpec((rows, TILE), lambda step, live: (0, step)), tile],
            out_specs=(pl.BlockSpec((rows, columns), lambda step, live: (0, 0)), tile, tile),
        ),
        compiler_params=pltpu.CompilerParams(vmem_limit_bytes=16 * MIB),
        cost_estimate=pl.CostEstimate(
            flops=2 * rows * TILE * columns * steps,
            bytes_accessed=4 * rows * (steps * TILE + columns),
            transcendentals=0,
        ),
    )(live, left, right)


def product_kernel(layout, added, scalars, *refs):
    count = len(layout)
    left_refs, refs = refs[: sum(layout)], refs[sum(layout) :]
    (high_ref, low_ref), refs = refs[:2], refs[2:]
    added_ref, (out_ref, *lefts) = (refs[0], refs[1:]) if added else (None, refs)
    lefts, (high, low, left_sems, sems) = lefts[:count], lefts[count:]
    steps = high.shape[0]

    left_copies = []
    for i, candidates in enumerate(layout):
        here, left_refs = left_refs[:candidates], left_refs[candidates:]
        copies = [pltpu.make_async_copy(ref, lefts[i], left_sems.at[i]) for ref in here]
        if candidates == 1:
            copies[0].start()
        else:
            for which, copy in enumerate(copies):
                pl.when(scalars[0] == which)(copy.start)
        left_copies.append(copies[0])
    right_copies = []
    for step in range(steps):
        pairs = (high_ref, high), (low_ref, low)
        right_copies.append(
            [
                pltpu.make_async_copy(source.at[step], target.at[step], sems.at[i, step])
                for i, (source, target) in enumerate(pairs)
            ]
        )
        for copy in right_copies[-1]:
            copy.start()
    out_ref[...] = added_ref[...] if added else jnp.zeros_like(out_ref)

    step = 0
    for i, left in enumerate(lefts):
        left_copies[i].wait()
        for tile in range(left.shape[1] // TILE):
            for copy in right_copies[step]:
                copy.wait()

            @pl.when(scalars[1 + step] > 0)
            def _():
                left_tile = left[:, tile * TILE : (tile + 1) * TILE]
                multiply_add(out_ref, left_tile, high[step], low[step])

            step += 1


def product(lists, which, right, live, added=None):
    rows, columns = lists[0][0].shape[0], right[0].shape[2]
    widths = [candidates[0].shape[1] for candidates in lists]
    steps = sum(widths) // TILE
    lefts = [x for candidates in lists for x in candidates]
    anywhere, vmem = (pl.BlockSpec(memory_space=space) for space in (pl.ANY, pltpu.VMEM))
    more = [] if added is None else [added]
    return pl.pallas_call(
        functools.partial(product_kernel, [len(candidates) for candidates in lists], added is not None),
        out_shape=jax.ShapeDtypeStruct((rows, columns), jnp.float32),
        in_specs=[pl.BlockSpec(memory_space=pltpu.SMEM)]
        + [anywhere] * (len(lefts) + 2)
        + [vmem] * len(more),
        out_specs=pl.BlockSpec(memory_space=pltpu.VMEM),
        scratch_shapes=[pltpu.VMEM((rows, width), jnp.float32) for width in widths]
        + [
            pltpu.VMEM((steps, TILE, columns), jnp.bfloat16),
            pltpu.VMEM((steps, TILE, columns), jnp.bfloat16),
            pltpu.SemaphoreType.DMA((len(lists),)),
            pltpu.SemaphoreType.DMA((2, steps)),
        ],
        compiler_params=pltpu.CompilerParams(vmem_limit_bytes=(52 if steps > 2 else 10) * MIB),
        cost_estimate=pl.CostEstimate(
            flops=2 * rows * TILE * columns * steps,
            bytes_accessed=4 * rows * (steps * TILE + columns),
            transcendentals=0,
        ),
    )(jnp.concatenate([jnp.int32(which)[None], live[:steps]]), *lefts, *right, *more)


def cut(left, tiles):
    kept = (tiles - tiles // 4) * TILE
    return [left[:, :kept], left[:, kept:]]


def take(blocks, at, axis):
    return lax.dynamic_index_in_dim(blocks, at, axis, keepdims=False)


def halve(blocks, axis, bit):
    mine = (lax.axis_index("cd") >> bit) & 1
    pairs = [(i, i ^ (1 << bit)) for i in range(lax.axis_size("cd"))]
    return take(blocks, mine, axis) + lax.ppermute(take(blocks, 1 - mine, axis), "cd", pairs)


def core_sum(partial_rows):
    count = lax.axis_size("cd")
    rows, columns = partial_rows.shape
    return halve(partial_rows.reshape(count // 2, 2, rows // count, columns), 1, 0)


def chip_sum(blocks):
    bit = 1
    while blocks.shape[0] > 1:
        chips, rows, columns = blocks.shape
        blocks = halve(blocks.reshape(chips // 2, 2, rows, columns), 1, bit)
        bit += 1
    return blocks[0]


def chip_sum_direct(blocks):
    chip, count = lax.axis_index("cd") // 2, lax.axis_size("cd")
    total = take(blocks, chip, 0)
    for flip in range(1, blocks.shape[0]):
        pairs = [(i, i ^ (2 * flip)) for i in range(count)]
        total += lax.ppermute(take(blocks, chip ^ flip, 0), "cd", pairs)
    return total


def send(x, pairs):
    return lax.ppermute(x, "ab", pairs)


def after(*values):
    return lax.optimization_barrier(values)


def ladder_any(amplitudes, live, right):
    count = lax.axis_size("ab")
    first, *split_right = first_product(amplitudes, right, live)
    home = [chip_sum(core_sum(first))]
    for flip in range(1, count):
        pairs = [(i, i ^ flip) for i in range(count)]
        lists = [[send(x, pairs)] for x in cut(amplitudes, live.shape[0])]
        partial_rows = product(lists, 0, split_right, live)
        home.append(send(chip_sum(core_sum(partial_rows)), pairs))
    return [take(jnp.stack(home), lax.axis_index("ab") ^ i, 0) for i in range(count)]


def ladder_line(amplitudes, live, right):
    at = lax.axis_index("ab")
    inner = ((at == 1) | (at == 2)).astype(jnp.int32)
    swap_1 = [(0, 1), (1, 0), (2, 3), (3, 2)]
    swap_2 = [(0, 2), (2, 0), (1, 3), (3, 1)]
    swap_3 = [(0, 3), (3, 0), (1, 2), (2, 1)]
    swap_inner, to_end = [(1, 2), (2, 1)], [(1, 0), (2, 3)]
    lists = cut(amplitudes, live.shape[0])
    kept = lists[0].shape[1] // TILE

    one = [send(x, swap_1) for x in lists]
    three_inner = [send(x, swap_inner) for x in lists]
    two_inner = [send(x, swap_inner) for x in one]
    two_end = [send(x, to_end) for x in three_inner]
    three_end = [send(x, to_end) for x in two_inner]

    first, *split_right = first_product(amplitudes, right, live)
    sum_0 = core_sum(first)

    one[0], three_inner[0], sum_0 = after(one[0], three_inner[0], sum_0)
    one[1], three_inner[1], sum_0 = after(one[1], three_inner[1], sum_0)
    sum_1 = core_sum(product([[x] for x in one], 0, split_right, live))
    home_0 = chip_sum(sum_0)

    two_end[0], two_inner[0], home_0, sum_1 = after(two_end[0], two_inner[0], home_0, sum_1)
    two_end[1], two_inner[1], sum_1 = after(two_end[1], two_inner[1], sum_1)
    candidates = [list(pair) for pair in zip(two_end, two_inner)]
    sum_2 = core_sum(product(candidates, inner, split_right, live))
    sum_1 = chip_sum(sum_1)

    last_right = [x[kept:] for x in split_right]

    three_end[0], sum_1, sum_2, last_right = after(three_end[0], sum_1, sum_2, last_right)
    candidates = [[three_end[0], three_inner[0]]]
    partial_3 = product(candidates, inner, split_right, live)
    sum_2 = chip_sum_direct(sum_2)

    three_end[1], partial_3, sum_2 = after(three_end[1], partial_3, sum_2)
    candidates = [[three_end[1], three_inner[1]]]
    partial_3 = product(candidates, inner, last_right, live[kept:], partial_3)
    sum_3 = chip_sum_direct(core_sum(partial_3))
    home_1, home_2 = send(sum_1, swap_1), send(sum_2, swap_2)

    home_1, home_2, sum_3 = after(home_1, home_2, sum_3)
    home = jnp.stack([home_0, home_1, home_2, send(sum_3, swap_3)])
    return [take(home, at ^ i, 0) for i in range(4)]


def per_device(amplitudes, integrals, live_tiles, residual_in):
    right = integrals.reshape(live_tiles.shape[0], TILE, integrals.shape[1])
    ladder = ladder_line if lax.axis_size("ab") == 4 else ladder_any
    return residual_in + jnp.concatenate(ladder(amplitudes, live_tiles, right), axis=1)


def solution(mesh):
    return jax.shard_map(
        per_device,
        mesh=mesh,
        in_specs=(P("ab", "cd"), P("cd", "ab"), P("cd"), P(("ab", "cd"), None)),
        out_specs=P(("ab", "cd"), None),
        check_vma=False,
    )
```

```python
import functools

import jax
import jax.numpy as jnp
from jax import lax
from jax.experimental import pallas as pl
from jax.experimental.pallas import tpu as pltpu
from jax.sharding import PartitionSpec as P

TILE = 256
MIB = 1 << 20


def split(x):
    high = x.astype(jnp.bfloat16)
    return high, (x - high.astype(jnp.float32)).astype(jnp.bfloat16)


def multiply_add(out_ref, left, high, low):
    left_high, left_low = split(left)
    dot = functools.partial(jnp.dot, preferred_element_type=jnp.float32)
    both = dot(jnp.concatenate([left_high, left_low]), high)
    rows = left.shape[0]
    out_ref[...] += both[:rows] + (both[rows:] + dot(left_high, low))


def first_kernel(live, left_ref, right_ref, out_ref, high_ref, low_ref):
    step = pl.program_id(0)

    @pl.when(step == 0)
    def _():
        out_ref[...] = jnp.zeros_like(out_ref)

    @pl.when(live[step] > 0)
    def _():
        high_ref[0], low_ref[0] = split(right_ref[0])
        multiply_add(out_ref, left_ref[...], high_ref[0], low_ref[0])

    @pl.when(live[step] == 0)
    def _():
        high_ref[...] = jnp.zeros_like(high_ref)
        low_ref[...] = jnp.zeros_like(low_ref)


def first_product(left, right, live):
    rows = left.shape[0]
    steps, _, columns = right.shape
    tile = pl.BlockSpec((1, TILE, columns), lambda step, live: (step, 0, 0))
    halved = jax.ShapeDtypeStruct(right.shape, jnp.bfloat16)
    return pl.pallas_call(
        first_kernel,
        out_shape=(jax.ShapeDtypeStruct((rows, columns), jnp.float32), halved, halved),
        grid_spec=pltpu.PrefetchScalarGridSpec(
            num_scalar_prefetch=1,
            grid=(steps,),
            in_specs=[pl.BlockSpec((rows, TILE), lambda step, live: (0, step)), tile],
            out_specs=(pl.BlockSpec((rows, columns), lambda step, live: (0, 0)), tile, tile),
        ),
        compiler_params=pltpu.CompilerParams(vmem_limit_bytes=16 * MIB),
        cost_estimate=pl.CostEstimate(
            flops=2 * rows * TILE * columns * steps,
            bytes_accessed=4 * rows * (steps * TILE + columns),
            transcendentals=0,
        ),
    )(live, left, right)


def product_kernel(layout, added, scalars, *refs):
    count = len(layout)
    left_refs, refs = refs[: sum(layout)], refs[sum(layout) :]
    (high_ref, low_ref), refs = refs[:2], refs[2:]
    added_ref, (out_ref, *lefts) = (refs[0], refs[1:]) if added else (None, refs)
    lefts, (high, low, left_sems, sems) = lefts[:count], lefts[count:]
    steps = high.shape[0]

    left_copies = []
    for i, candidates in enumerate(layout):
        here, left_refs = left_refs[:candidates], left_refs[candidates:]
        copies = [pltpu.make_async_copy(ref, lefts[i], left_sems.at[i]) for ref in here]
        if candidates == 1:
            copies[0].start()
        else:
            for which, copy in enumerate(copies):
                pl.when(scalars[0] == which)(copy.start)
        left_copies.append(copies[0])
    right_copies = []
    for step in range(steps):
        pairs = (high_ref, high), (low_ref, low)
        right_copies.append(
            [
                pltpu.make_async_copy(source.at[step], target.at[step], sems.at[i, step])
                for i, (source, target) in enumerate(pairs)
            ]
        )
        for copy in right_copies[-1]:
            copy.start()
    out_ref[...] = added_ref[...] if added else jnp.zeros_like(out_ref)

    step = 0
    for i, left in enumerate(lefts):
        left_copies[i].wait()
        tiles = left.shape[1] // TILE
        for tile in range(0, tiles, 2):
            count = min(2, tiles - tile)
            for copy in right_copies[step : step + count]:
                copy[0].wait()
                copy[1].wait()
            alive = [scalars[1 + step + j] for j in range(count)]

            @pl.when(sum(alive) > 0)
            def _():
                pieces = [left[:, (tile + j) * TILE : (tile + j + 1) * TILE] for j in range(count)]
                pieces = [jnp.where(x > 0, piece, 0.0) for x, piece in zip(alive, pieces)]
                rights = [x[step : step + count].reshape(count * TILE, -1) for x in (high, low)]
                multiply_add(out_ref, jnp.concatenate(pieces, axis=1), *rights)

            step += count


def product(lists, which, right, live, added=None):
    rows, columns = lists[0][0].shape[0], right[0].shape[2]
    widths = [candidates[0].shape[1] for candidates in lists]
    steps = sum(widths) // TILE
    lefts = [x for candidates in lists for x in candidates]
    anywhere, vmem = (pl.BlockSpec(memory_space=space) for space in (pl.ANY, pltpu.VMEM))
    more = [] if added is None else [added]
    return pl.pallas_call(
        functools.partial(product_kernel, [len(candidates) for candidates in lists], added is not None),
        out_shape=jax.ShapeDtypeStruct((rows, columns), jnp.float32),
        in_specs=[pl.BlockSpec(memory_space=pltpu.SMEM)]
        + [anywhere] * (len(lefts) + 2)
        + [vmem] * len(more),
        out_specs=pl.BlockSpec(memory_space=pltpu.VMEM),
        scratch_shapes=[pltpu.VMEM((rows, width), jnp.float32) for width in widths]
        + [
            pltpu.VMEM((steps, TILE, columns), jnp.bfloat16),
            pltpu.VMEM((steps, TILE, columns), jnp.bfloat16),
            pltpu.SemaphoreType.DMA((len(lists),)),
            pltpu.SemaphoreType.DMA((2, steps)),
        ],
        compiler_params=pltpu.CompilerParams(vmem_limit_bytes=(52 if steps > 2 else 10) * MIB),
        cost_estimate=pl.CostEstimate(
            flops=2 * rows * TILE * columns * steps,
            bytes_accessed=4 * rows * (steps * TILE + columns),
            transcendentals=0,
        ),
    )(jnp.concatenate([jnp.int32(which)[None], live[:steps]]), *lefts, *right, *more)


def cut(left, tiles):
    kept = (tiles - tiles // 4) * TILE
    return [left[:, :kept], left[:, kept:]]


def take(blocks, at, axis):
    return lax.dynamic_index_in_dim(blocks, at, axis, keepdims=False)


def halve(blocks, axis, bit):
    mine = (lax.axis_index("cd") >> bit) & 1
    pairs = [(i, i ^ (1 << bit)) for i in range(lax.axis_size("cd"))]
    return take(blocks, mine, axis) + lax.ppermute(take(blocks, 1 - mine, axis), "cd", pairs)


def core_sum(partial_rows):
    count = lax.axis_size("cd")
    rows, columns = partial_rows.shape
    return halve(partial_rows.reshape(count // 2, 2, rows // count, columns), 1, 0)


def chip_sum(blocks):
    bit = 1
    while blocks.shape[0] > 1:
        chips, rows, columns = blocks.shape
        blocks = halve(blocks.reshape(chips // 2, 2, rows, columns), 1, bit)
        bit += 1
    return blocks[0]


def chip_sum_direct(blocks):
    chip, count = lax.axis_index("cd") // 2, lax.axis_size("cd")
    total = take(blocks, chip, 0)
    for flip in range(1, blocks.shape[0]):
        pairs = [(i, i ^ (2 * flip)) for i in range(count)]
        total += lax.ppermute(take(blocks, chip ^ flip, 0), "cd", pairs)
    return total


def send(x, pairs):
    return lax.ppermute(x, "ab", pairs)


def after(*values):
    return lax.optimization_barrier(values)


def ladder_any(amplitudes, live, right):
    count = lax.axis_size("ab")
    first, *split_right = first_product(amplitudes, right, live)
    home = [chip_sum(core_sum(first))]
    for flip in range(1, count):
        pairs = [(i, i ^ flip) for i in range(count)]
        lists = [[send(x, pairs)] for x in cut(amplitudes, live.shape[0])]
        partial_rows = product(lists, 0, split_right, live)
        home.append(send(chip_sum(core_sum(partial_rows)), pairs))
    return [take(jnp.stack(home), lax.axis_index("ab") ^ i, 0) for i in range(count)]


def ladder_line(amplitudes, live, right):
    at = lax.axis_index("ab")
    inner = ((at == 1) | (at == 2)).astype(jnp.int32)
    swap_1 = [(0, 1), (1, 0), (2, 3), (3, 2)]
    swap_2 = [(0, 2), (2, 0), (1, 3), (3, 1)]
    swap_3 = [(0, 3), (3, 0), (1, 2), (2, 1)]
    swap_inner, to_end = [(1, 2), (2, 1)], [(1, 0), (2, 3)]
    lists = cut(amplitudes, live.shape[0])
    kept = lists[0].shape[1] // TILE

    one = [send(x, swap_1) for x in lists]
    three_inner = [send(x, swap_inner) for x in lists]
    two_inner = [send(x, swap_inner) for x in one]
    two_end = [send(x, to_end) for x in three_inner]
    three_end = [send(x, to_end) for x in two_inner]

    first, *split_right = first_product(amplitudes, right, live)
    sum_0 = core_sum(first)

    one[0], three_inner[0], sum_0 = after(one[0], three_inner[0], sum_0)
    one[1], three_inner[1], sum_0 = after(one[1], three_inner[1], sum_0)
    sum_1 = core_sum(product([[x] for x in one], 0, split_right, live))
    home_0 = chip_sum(sum_0)

    two_end[0], two_inner[0], home_0, sum_1 = after(two_end[0], two_inner[0], home_0, sum_1)
    two_end[1], two_inner[1], sum_1 = after(two_end[1], two_inner[1], sum_1)
    candidates = [list(pair) for pair in zip(two_end, two_inner)]
    sum_2 = core_sum(product(candidates, inner, split_right, live))
    sum_1 = chip_sum(sum_1)

    last_right = [x[kept:] for x in split_right]

    three_end[0], sum_1, sum_2, last_right = after(three_end[0], sum_1, sum_2, last_right)
    candidates = [[three_end[0], three_inner[0]]]
    partial_3 = product(candidates, inner, split_right, live)
    sum_2 = chip_sum_direct(sum_2)

    three_end[1], partial_3, sum_2 = after(three_end[1], partial_3, sum_2)
    candidates = [[three_end[1], three_inner[1]]]
    partial_3 = product(candidates, inner, last_right, live[kept:], partial_3)
    sum_3 = chip_sum_direct(core_sum(partial_3))
    home_1, home_2 = send(sum_1, swap_1), send(sum_2, swap_2)

    home_1, home_2, sum_3 = after(home_1, home_2, sum_3)
    home = jnp.stack([home_0, home_1, home_2, send(sum_3, swap_3)])
    return [take(home, at ^ i, 0) for i in range(4)]


def per_device(amplitudes, integrals, live_tiles, residual_in):
    right = integrals.reshape(live_tiles.shape[0], TILE, integrals.shape[1])
    ladder = ladder_line if lax.axis_size("ab") == 4 else ladder_any
    return residual_in + jnp.concatenate(ladder(amplitudes, live_tiles, right), axis=1)


def solution(mesh):
    return jax.shard_map(
        per_device,
        mesh=mesh,
        in_specs=(P("ab", "cd"), P("cd", "ab"), P("cd"), P(("ab", "cd"), None)),
        out_specs=P(("ab", "cd"), None),
        check_vma=False,
    )
```

```python
import functools

import jax
import jax.numpy as jnp
from jax import lax
from jax.experimental import pallas as pl
from jax.experimental.pallas import tpu as pltpu
from jax.sharding import PartitionSpec as P

TILE = 256
MIB = 1 << 20


def split(x):
    high = x.astype(jnp.bfloat16)
    return high, (x - high.astype(jnp.float32)).astype(jnp.bfloat16)


def multiply_add(out_ref, left, high, low):
    left_high, left_low = split(left)
    dot = functools.partial(jnp.dot, preferred_element_type=jnp.float32)
    both = dot(jnp.concatenate([left_high, left_low]), high)
    rows = left.shape[0]
    out_ref[...] += both[:rows] + (both[rows:] + dot(left_high, low))


def first_kernel(live, left_ref, right_ref, out_ref, high_ref, low_ref):
    step = pl.program_id(0)

    @pl.when(step == 0)
    def _():
        out_ref[...] = jnp.zeros_like(out_ref)

    @pl.when(live[step] > 0)
    def _():
        high_ref[0], low_ref[0] = split(right_ref[0])
        multiply_add(out_ref, left_ref[...], high_ref[0], low_ref[0])

    @pl.when(live[step] == 0)
    def _():
        high_ref[...] = jnp.zeros_like(high_ref)
        low_ref[...] = jnp.zeros_like(low_ref)


def first_product(left, right, live):
    rows = left.shape[0]
    steps, _, columns = right.shape
    tile = pl.BlockSpec((1, TILE, columns), lambda step, live: (step, 0, 0))
    halved = jax.ShapeDtypeStruct(right.shape, jnp.bfloat16)
    return pl.pallas_call(
        first_kernel,
        out_shape=(jax.ShapeDtypeStruct((rows, columns), jnp.float32), halved, halved),
        grid_spec=pltpu.PrefetchScalarGridSpec(
            num_scalar_prefetch=1,
            grid=(steps,),
            in_specs=[pl.BlockSpec((rows, TILE), lambda step, live: (0, step)), tile],
            out_specs=(pl.BlockSpec((rows, columns), lambda step, live: (0, 0)), tile, tile),
        ),
        compiler_params=pltpu.CompilerParams(vmem_limit_bytes=16 * MIB),
        cost_estimate=pl.CostEstimate(
            flops=2 * rows * TILE * columns * steps,
            bytes_accessed=4 * rows * (steps * TILE + columns),
            transcendentals=0,
        ),
    )(live, left, right)


def product_kernel(layout, added, scalars, *refs):
    count = len(layout)
    left_refs, refs = refs[: sum(layout)], refs[sum(layout) :]
    (high_ref, low_ref), refs = refs[:2], refs[2:]
    added_ref, (out_ref, *lefts) = (refs[0], refs[1:]) if added else (None, refs)
    lefts, (high, low, left_sems, sems) = lefts[:count], lefts[count:]
    steps = high.shape[0]

    left_copies = []
    for i, candidates in enumerate(layout):
        here, left_refs = left_refs[:candidates], left_refs[candidates:]
        copies = [pltpu.make_async_copy(ref, lefts[i], left_sems.at[i]) for ref in here]
        if candidates == 1:
            copies[0].start()
        else:
            for which, copy in enumerate(copies):
                pl.when(scalars[0] == which)(copy.start)
        left_copies.append(copies[0])
    right_copies = []
    for step in range(steps):
        pairs = (high_ref, high), (low_ref, low)
        right_copies.append(
            [
                pltpu.make_async_copy(source.at[step], target.at[step], sems.at[i, step])
                for i, (source, target) in enumerate(pairs)
            ]
        )
        for copy in right_copies[-1]:
            copy.start()
    out_ref[...] = added_ref[...] if added else jnp.zeros_like(out_ref)

    step = 0
    for i, left in enumerate(lefts):
        left_copies[i].wait()
        tiles = left.shape[1] // TILE
        for tile in range(0, tiles, 2):
            count = min(2, tiles - tile)
            for copy in right_copies[step : step + count]:
                copy[0].wait()
                copy[1].wait()
            alive = [scalars[1 + step + j] for j in range(count)]

            @pl.when(sum(alive) > 0)
            def _():
                pieces = [left[:, (tile + j) * TILE : (tile + j + 1) * TILE] for j in range(count)]
                pieces = [jnp.where(x > 0, piece, 0.0) for x, piece in zip(alive, pieces)]
                rights = [x[step : step + count].reshape(count * TILE, -1) for x in (high, low)]
                multiply_add(out_ref, jnp.concatenate(pieces, axis=1), *rights)

            step += count


def product(lists, which, right, live, added=None):
    rows, columns = lists[0][0].shape[0], right[0].shape[2]
    widths = [candidates[0].shape[1] for candidates in lists]
    steps = sum(widths) // TILE
    lefts = [x for candidates in lists for x in candidates]
    anywhere, vmem = (pl.BlockSpec(memory_space=space) for space in (pl.ANY, pltpu.VMEM))
    more = [] if added is None else [added]
    return pl.pallas_call(
        functools.partial(product_kernel, [len(candidates) for candidates in lists], added is not None),
        out_shape=jax.ShapeDtypeStruct((rows, columns), jnp.float32),
        in_specs=[pl.BlockSpec(memory_space=pltpu.SMEM)]
        + [anywhere] * (len(lefts) + 2)
        + [vmem] * len(more),
        out_specs=pl.BlockSpec(memory_space=pltpu.VMEM),
        scratch_shapes=[pltpu.VMEM((rows, width), jnp.float32) for width in widths]
        + [
            pltpu.VMEM((steps, TILE, columns), jnp.bfloat16),
            pltpu.VMEM((steps, TILE, columns), jnp.bfloat16),
            pltpu.SemaphoreType.DMA((len(lists),)),
            pltpu.SemaphoreType.DMA((2, steps)),
        ],
        compiler_params=pltpu.CompilerParams(vmem_limit_bytes=(52 if steps > 2 else 10) * MIB),
        cost_estimate=pl.CostEstimate(
            flops=2 * rows * TILE * columns * steps,
            bytes_accessed=4 * rows * (steps * TILE + columns),
            transcendentals=0,
        ),
    )(jnp.concatenate([jnp.int32(which)[None], live[:steps]]), *lefts, *right, *more)


def cut(left, tiles):
    kept = (tiles - tiles // 4) * TILE
    return [left[:, :kept], left[:, kept:]]


def cut_kernel(left_ref, *refs):
    *list_refs, sems = refs
    copies, first = [], 0
    for i, list_ref in enumerate(list_refs):
        width = list_ref.shape[1]
        source = left_ref.at[:, pl.ds(first, width)]
        copies.append(pltpu.make_async_copy(source, list_ref, sems.at[i]))
        copies[-1].start()
        first += width
    for copy in copies:
        copy.wait()


def cut_argument(left, tiles):
    rows, columns = left.shape
    kept = (tiles - tiles // 4) * TILE
    widths = [kept, columns - kept]
    return pl.pallas_call(
        cut_kernel,
        out_shape=[jax.ShapeDtypeStruct((rows, width), left.dtype) for width in widths],
        in_specs=[pl.BlockSpec(memory_space=pl.ANY)],
        out_specs=[pl.BlockSpec(memory_space=pltpu.VMEM)] * 2,
        scratch_shapes=[pltpu.SemaphoreType.DMA((2,))],
        compiler_params=pltpu.CompilerParams(vmem_limit_bytes=52 * MIB),
    )(left)


def take(blocks, at, axis):
    return lax.dynamic_index_in_dim(blocks, at, axis, keepdims=False)


def halve(blocks, axis, bit):
    mine = (lax.axis_index("cd") >> bit) & 1
    pairs = [(i, i ^ (1 << bit)) for i in range(lax.axis_size("cd"))]
    return take(blocks, mine, axis) + lax.ppermute(take(blocks, 1 - mine, axis), "cd", pairs)


def core_sum(partial_rows):
    count = lax.axis_size("cd")
    rows, columns = partial_rows.shape
    return halve(partial_rows.reshape(count // 2, 2, rows // count, columns), 1, 0)


def chip_sum(blocks):
    bit = 1
    while blocks.shape[0] > 1:
        chips, rows, columns = blocks.shape
        blocks = halve(blocks.reshape(chips // 2, 2, rows, columns), 1, bit)
        bit += 1
    return blocks[0]


def chip_sum_direct(blocks):
    chip, count = lax.axis_index("cd") // 2, lax.axis_size("cd")
    total = take(blocks, chip, 0)
    for flip in range(1, blocks.shape[0]):
        pairs = [(i, i ^ (2 * flip)) for i in range(count)]
        total += lax.ppermute(take(blocks, chip ^ flip, 0), "cd", pairs)
    return total


def send(x, pairs):
    return lax.ppermute(x, "ab", pairs)


def after(*values):
    return lax.optimization_barrier(values)


def ladder_any(amplitudes, live, right):
    count = lax.axis_size("ab")
    first, *split_right = first_product(amplitudes, right, live)
    home = [chip_sum(core_sum(first))]
    for flip in range(1, count):
        pairs = [(i, i ^ flip) for i in range(count)]
        lists = [[send(x, pairs)] for x in cut(amplitudes, live.shape[0])]
        partial_rows = product(lists, 0, split_right, live)
        home.append(send(chip_sum(core_sum(partial_rows)), pairs))
    return [take(jnp.stack(home), lax.axis_index("ab") ^ i, 0) for i in range(count)]


def ladder_line(amplitudes, live, right):
    at = lax.axis_index("ab")
    inner = ((at == 1) | (at == 2)).astype(jnp.int32)
    swap_1 = [(0, 1), (1, 0), (2, 3), (3, 2)]
    swap_2 = [(0, 2), (2, 0), (1, 3), (3, 1)]
    swap_3 = [(0, 3), (3, 0), (1, 2), (2, 1)]
    swap_inner, to_end = [(1, 2), (2, 1)], [(1, 0), (2, 3)]
    lists = cut_argument(amplitudes, live.shape[0])
    kept = lists[0].shape[1] // TILE

    one = [send(x, swap_1) for x in lists]
    three_inner = [send(x, swap_inner) for x in lists]
    two_inner = [send(x, swap_inner) for x in one]
    two_end = [send(x, to_end) for x in three_inner]
    three_end = [send(x, to_end) for x in two_inner]

    first, *split_right = first_product(amplitudes, right, live)
    sum_0 = core_sum(first)

    one[0], three_inner[0], sum_0 = after(one[0], three_inner[0], sum_0)
    one[1], three_inner[1], sum_0 = after(one[1], three_inner[1], sum_0)
    sum_1 = core_sum(product([[x] for x in one], 0, split_right, live))
    home_0 = chip_sum(sum_0)

    two_end[0], two_inner[0], home_0, sum_1 = after(two_end[0], two_inner[0], home_0, sum_1)
    two_end[1], two_inner[1], sum_1 = after(two_end[1], two_inner[1], sum_1)
    candidates = [list(pair) for pair in zip(two_end, two_inner)]
    sum_2 = core_sum(product(candidates, inner, split_right, live))
    sum_1 = chip_sum(sum_1)

    last_right = [x[kept:] for x in split_right]

    three_end[0], sum_1, sum_2, last_right = after(three_end[0], sum_1, sum_2, last_right)
    candidates = [[three_end[0], three_inner[0]]]
    partial_3 = product(candidates, inner, split_right, live)
    sum_2 = chip_sum_direct(sum_2)

    three_end[1], partial_3, sum_2 = after(three_end[1], partial_3, sum_2)
    candidates = [[three_end[1], three_inner[1]]]
    partial_3 = product(candidates, inner, last_right, live[kept:], partial_3)
    sum_3 = chip_sum_direct(core_sum(partial_3))
    home_1, home_2 = send(sum_1, swap_1), send(sum_2, swap_2)

    home_1, home_2, sum_3 = after(home_1, home_2, sum_3)
    home = jnp.stack([home_0, home_1, home_2, send(sum_3, swap_3)])
    return [take(home, at ^ i, 0) for i in range(4)]


def per_device(amplitudes, integrals, live_tiles, residual_in):
    right = integrals.reshape(live_tiles.shape[0], TILE, integrals.shape[1])
    ladder = ladder_line if lax.axis_size("ab") == 4 else ladder_any
    return residual_in + jnp.concatenate(ladder(amplitudes, live_tiles, right), axis=1)


def solution(mesh):
    return jax.shard_map(
        per_device,
        mesh=mesh,
        in_specs=(P("ab", "cd"), P("cd", "ab"), P("cd"), P(("ab", "cd"), None)),
        out_specs=P(("ab", "cd"), None),
        check_vma=False,
    )
```
